32 devices in a mesh: dp: 2 (over x), ctx: 16 (over z, y, core).
Axes of the slice: x: 2, y: 2, z: 4, core: 2. Of those that a mesh axis runs over, the one named last changes fastest.
Arguments:
- queries: bfloat16 [4096, 2048], P(('dp', 'ctx')), parts along dimension 0, may hold values from -6 to 6
- key_rows: bfloat16 [4096, 2048], P(('dp', 'ctx')), parts along dimension 0, may hold values from -6 to 6
- value_rows: bfloat16 [4096, 2048], P(('dp', 'ctx')), parts along dimension 0, may hold values from -6 to 6
- attn_out: bfloat16 [4096, 2048], P(('dp', 'ctx')), parts along dimension 0, may hold values from -6 to 6
- out_grad: bfloat16 [4096, 2048], P(('dp', 'ctx')), parts along dimension 0, may hold values from -6 to 6
- log_norm: float32 [4096, 16], P(('dp', 'ctx')), parts along dimension 0, may hold values from 4 to 7
- segments: int32 [4096], P(('dp', 'ctx')), parts along dimension 0, may hold values from 0 to 7, never falling along the last dimension, each value on 1 to 896 neighbouring positions
Outputs:
- query_grad: bfloat16 [4096, 2048], P(('dp', 'ctx')), parts along dimension 0
- key_grad: bfloat16 [4096, 2048], P(('dp', 'ctx')), parts along dimension 0
- value_grad: bfloat16 [4096, 2048], P(('dp', 'ctx')), parts along dimension 0
The draws below stay inside these ranges and needn't reach their ends.
There are 2 independent parts, one for each index of `dp`. The reference program is written for one: setup_inputs(seed, part) draws one part's arguments, and reference() takes and returns one part's arrays. A program takes and returns all parts, laid end to end along the dimension named above; each array names one. Nothing has to cross between parts.
Inputs may be any that keep to these rules, and one draw needn't show every extreme that they name: `segments`: never falls along the tokens; every document number is used; no document has more than 896 tokens and one has exactly 896.
All inputs are finite; a program needn't handle non-finite values.
Results may differ from the reference program's by a relative error of at most 0.0085.
Values may be sent and summed in bfloat16 or wider, within the bound.
A program may use at most 64 MiB of HBM per device.

```python
import math
import jax
import jax.numpy as jnp
import numpy as np
from jax import lax

HEADS = 16
HEAD_DIM = 128
TOK_DEV = 128
SEQ_DEVS = 8
ROWS = 2048
DOCS = 8
DOC_MOST = 896


def levels(key, dims, split, smallest, largest):
    loudness = 1.0
    for position, parts in split:
        heights = jax.random.uniform(jax.random.fold_in(jax.random.fold_in(key, 6), position), (parts,), jnp.float32, smallest / len(split), largest / len(split))
        loudness = loudness * jnp.repeat(jnp.exp(heights), dims[position] // parts).reshape((-1,) + (1,) * (len(dims) - 1 - position))
    return loudness


def length_profile(number_of, total, limit, lean):
    portions = [(1 << 20) // math.isqrt(grade ** lean) + 1 for grade in range(2, number_of + 1)]
    rest, counts = total - limit - (number_of - 1), [1] * (number_of - 1)
    while rest > 0:
        candidates = [i for i in range(number_of - 1) if counts[i] < limit]
        pool, remaining = sum([portions[i] for i in candidates]), rest
        for i in candidates:
            more = min(limit - counts[i], max(1, remaining * portions[i] // pool), rest)
            counts[i] = counts[i] + more
            rest = rest - more
    return np.array([limit] + counts)


def uneven_parts(stream_key, number_of, total, limit, lean):
    if number_of == 2:
        one = jax.random.randint(stream_key, (), max(1, total - limit), min(limit, total - 1) + 1)
        return jnp.stack([one, total - one])
    sizes = jnp.asarray(length_profile(number_of, total, limit, lean), jnp.int32)
    pairs = (number_of - 1) // 2
    source_of, receiver = sizes[1:1 + 2 * pairs:2], sizes[2:2 + 2 * pairs:2]
    room = jnp.minimum(source_of - 1, limit - receiver)
    passed = jax.random.randint(jax.random.fold_in(stream_key, 1), (pairs,), 0, 1 << 20) % (room + 1)
    sizes = sizes.at[1:1 + 2 * pairs:2].set(source_of - passed).at[2:2 + 2 * pairs:2].set(receiver + passed)
    return sizes[jax.random.permutation(jax.random.fold_in(stream_key, 2), number_of)]


def scatter_about(rng, extent, deviation, bound, cuts=(), held_as=jnp.bfloat16):
    factor_of = levels(rng, extent, cuts, -0.22, 0.18) if cuts else 1.0
    values = jax.random.normal(rng, extent, jnp.float32) * deviation * factor_of
    return jnp.minimum(jnp.maximum(values, -bound), bound).astype(held_as)


def setup_inputs(seed: int = 0, part: int = 0) -> dict:
    splits = jax.random.split(jax.random.key(seed), 8)
    part_splits = jax.random.split(jax.random.fold_in(splits[7], part), 8)
    queries = scatter_about(part_splits[0], (ROWS, HEADS * HEAD_DIM), 1.0, 6.0, ((0, 16),))
    key_rows = scatter_about(part_splits[1], (ROWS, HEADS * HEAD_DIM), 1.0, 6.0, ((0, 16),))
    value_rows = scatter_about(part_splits[2], (ROWS, HEADS * HEAD_DIM), 1.0, 6.0, ((0, 16),))
    attn_out = scatter_about(part_splits[3], (ROWS, HEADS * HEAD_DIM), 1.0, 6.0, ((0, 16),))
    out_grad = scatter_about(part_splits[4], (ROWS, HEADS * HEAD_DIM), 1.0, 6.0, ((0, 16),))
    log_norm = jnp.clip(4.0 + 3.0 * jax.random.uniform(part_splits[5], (ROWS, HEADS), jnp.float32) ** levels(part_splits[5], (ROWS, HEADS), ((0, 16),), -0.2, 0.2), 4.0, 7.0)
    segments = jnp.searchsorted(jnp.cumsum(uneven_parts(part_splits[6], DOCS, ROWS, DOC_MOST, 2)), jnp.arange(ROWS), side="right").astype(jnp.int32)
    return dict(queries=queries, key_rows=key_rows, value_rows=value_rows, attn_out=attn_out, out_grad=out_grad, log_norm=log_norm, segments=segments)


def reference(queries, key_rows, value_rows, attn_out, out_grad, log_norm, segments):
    softmax_scale = HEAD_DIM ** -0.5
    seq_span = queries.shape[0]
    block_count = seq_span // TOK_DEV
    reach = (SEQ_DEVS - 1) * TOK_DEV
    window = SEQ_DEVS * TOK_DEV

    def as_heads(matrix):
        return matrix.reshape(seq_span, HEADS, HEAD_DIM)

    query_all = as_heads(queries)
    grad_all = as_heads(out_grad)
    row_delta = jnp.sum(grad_all.astype(jnp.float32) * as_heads(attn_out).astype(jnp.float32), axis=2)
    zero_pad = jnp.zeros((reach, HEADS, HEAD_DIM), jnp.bfloat16)
    key_pad = jnp.concatenate([zero_pad, as_heads(key_rows)], axis=0)
    value_pad = jnp.concatenate([zero_pad, as_heads(value_rows)], axis=0)
    seg_pad = jnp.concatenate([jnp.full((reach,), -1, jnp.int32), segments.astype(jnp.int32)], axis=0)

    def one_block(carry, block_id):
        key_total, value_total = carry
        start = (block_id * TOK_DEV).astype(jnp.int32)
        query_part = lax.dynamic_slice_in_dim(query_all, start, TOK_DEV, 0)
        grad_part = lax.dynamic_slice_in_dim(grad_all, start, TOK_DEV, 0)
        norm_part = lax.dynamic_slice_in_dim(log_norm, start, TOK_DEV, 0)
        delta_part = lax.dynamic_slice_in_dim(row_delta, start, TOK_DEV, 0)
        seg_query = lax.dynamic_slice_in_dim(segments.astype(jnp.int32), start, TOK_DEV, 0)
        key_part = lax.dynamic_slice_in_dim(key_pad, start, window, 0)
        value_part = lax.dynamic_slice_in_dim(value_pad, start, window, 0)
        seg_key = lax.dynamic_slice_in_dim(seg_pad, start, window, 0)
        query_pos = start + jnp.arange(TOK_DEV, dtype=jnp.int32)
        key_pos = start - reach + jnp.arange(window, dtype=jnp.int32)
        allowed = (seg_query[:, None] == seg_key[None, :]) & (key_pos[None, :] <= query_pos[:, None])
        scores = jnp.einsum("qhd,khd->hqk", query_part.astype(jnp.float32), key_part.astype(jnp.float32)) * softmax_scale
        attn_prob = jnp.where(allowed[None], jnp.exp(scores - norm_part.T[:, :, None]), 0.0)
        prob_low = lax.optimization_barrier(attn_prob.astype(jnp.bfloat16))
        value_add = jnp.einsum("hqk,qhd->khd", prob_low.astype(jnp.float32), grad_part.astype(jnp.float32))
        prob_grad = jnp.einsum("qhd,khd->hqk", grad_part.astype(jnp.float32), value_part.astype(jnp.float32))
        score_low = lax.optimization_barrier((attn_prob * (prob_grad - delta_part.T[:, :, None])).astype(jnp.bfloat16))
        query_grad = softmax_scale * jnp.einsum("hqk,khd->qhd", score_low.astype(jnp.float32), key_part.astype(jnp.float32))
        key_add = jnp.einsum("hqk,qhd->khd", score_low.astype(jnp.float32), query_part.astype(jnp.float32))
        key_total = lax.dynamic_update_slice_in_dim(key_total, lax.dynamic_slice_in_dim(key_total, start, window, 0) + key_add, start, 0)
        value_total = lax.dynamic_update_slice_in_dim(value_total, lax.dynamic_slice_in_dim(value_total, start, window, 0) + value_add, start, 0)
        return (key_total, value_total), query_grad.astype(jnp.bfloat16)

    empty = jnp.zeros((seq_span + reach, HEADS, HEAD_DIM), jnp.float32)
    (key_total, value_total), query_blocks = lax.scan(one_block, (empty, empty), jnp.arange(block_count, dtype=jnp.int32))
    query_grad = query_blocks.reshape(queries.shape)
    key_grad = (softmax_scale * key_total[reach:]).astype(jnp.bfloat16).reshape(queries.shape)
    value_grad = value_total[reach:].astype(jnp.bfloat16).reshape(queries.shape)
    return query_grad, key_grad, value_grad
```

```python
import functools

import jax
import jax.numpy as jnp
from jax import lax
from jax.experimental import pallas as pl
from jax.experimental.pallas import tpu as pltpu
from jax.sharding import PartitionSpec as P

HEAD_DIM = 128
SEQ_DEVS = 8
GROUP = 4
LOG2E = 1.4426950408889634
MESH = pl.DeviceIdType.MESH
SCALE = HEAD_DIM ** (-0.5)


def dot(a, b, a_dim, b_dim):
    return lax.dot_general(a, b, (((a_dim,), (b_dim,)), ((), ())), preferred_element_type=jnp.float32)


def kernel(
    chain_len,
    q_ref, k_ref, v_ref, o_ref, g_ref, ln_ref, seg_ref,
    dq_ref, dk_ref, dv_ref,
    stat_send, visit, stat, keys, values, key_seg, dk_acc, dv_acc, dq_acc,
    dq_send, dq_recv, out_send,
    in_ssem, in_rsem, hop_ssem, hop_rsem, dq_ssem, dq_rsem, out_ssem, out_rsem,
):
    tok = q_ref.shape[0]
    cols = q_ref.shape[1] // GROUP
    heads = cols // HEAD_DIM
    me = lax.axis_index("ctx")
    layer = me // GROUP
    place = me % GROUP
    layers = chain_len // GROUP
    base = layer * GROUP
    flip = place + 1 - 2 * (place % 2)
    order = [place, flip, (place + 2) % GROUP, (flip + 2) % GROUP]
    prev1, prev2 = layer >= 1, layer >= 2
    next1, next2 = layer <= layers - 2, layer <= layers - 3

    def part(p):
        return pl.ds(pl.multiple_of(p * cols, cols), cols)

    def rows_of(b):
        return pl.ds(pl.multiple_of(b * tok, tok), tok)

    def copy(src, dst, ssem, rsem, to):
        return pltpu.make_async_remote_copy(
            src_ref=src, dst_ref=dst, send_sem=ssem, recv_sem=rsem,
            device_id={"ctx": to}, device_id_type=MESH,
        )

    barrier = pltpu.get_barrier_semaphore()

    def greet(to):
        pl.semaphore_signal(barrier, inc=1, device_id={"ctx": to}, device_id_type=MESH)

    for r in range(1, GROUP):
        greet(base + order[r])
    for there, to in ((prev1, me - GROUP), (prev2, me - 2 * GROUP), (next1, me + GROUP), (next2, me + 2 * GROUP)):
        pl.when(there)(functools.partial(greet, to))

    visit[0, place, 0] = q_ref[:, part(place)]
    visit[0, place, 1] = g_ref[:, part(place)]
    keys[rows_of(place), :] = k_ref[:, part(place)]
    values[rows_of(place), :] = v_ref[:, part(place)]

    lane = lax.broadcasted_iota(jnp.int32, (tok, 128), 1)
    table = jnp.zeros((tok, 128), jnp.float32)
    for h in range(GROUP * heads):
        here = slice(h * HEAD_DIM, (h + 1) * HEAD_DIM)
        delta = jnp.sum(g_ref[:, here].astype(jnp.float32) * o_ref[:, here].astype(jnp.float32), axis=1, keepdims=True)
        at = (h // heads) * 16 + h % heads
        table = jnp.where(lane == at, delta, table)
        table = jnp.where(lane == at + heads, ln_ref[:, h : h + 1] * LOG2E, table)
    table = table.T
    seg_rows = jnp.broadcast_to(seg_ref[...].astype(jnp.float32), (8, tok))
    for p in range(GROUP):
        stat_send[p, 0:8, :] = table[16 * p : 16 * p + 8, :]
        stat_send[p, 8:16, :] = seg_rows
    stat[0, place] = stat_send[place]
    dk_acc[...] = jnp.zeros_like(dk_acc)
    dv_acc[...] = jnp.zeros_like(dv_acc)

    partners = 3 + prev1.astype(jnp.int32) + prev2.astype(jnp.int32) + next1.astype(jnp.int32) + next2.astype(jnp.int32)
    pl.semaphore_wait(barrier, partners)

    def in_copy(a, r, sending):
        p = order[r]
        at = place if sending else p
        src = (q_ref.at[:, part(p)], g_ref.at[:, part(p)], stat_send.at[p], k_ref.at[:, part(p)], v_ref.at[:, part(p)])[a]
        dst = (visit.at[0, at, 0], visit.at[0, at, 1], stat.at[0, at], keys.at[rows_of(at)], values.at[rows_of(at)])[a]
        return copy(src, dst, in_ssem.at[a, r], in_rsem.at[a, r], base + p)

    def hop_copies(hop, b):
        to = me - GROUP
        return (
            copy(visit.at[hop, b], visit.at[hop + 1, b], hop_ssem.at[hop, 0, b], hop_rsem.at[hop, 0, b], to),
            copy(stat.at[hop, b], stat.at[hop + 1, b], hop_ssem.at[hop, 1, b], hop_rsem.at[hop, 1, b], to),
        )

    def dq_copy(d, b):
        return copy(dq_send.at[d, b], dq_recv.at[d, b], dq_ssem.at[d, b], dq_rsem.at[d, b], me + (d + 1) * GROUP)

    def out_copy(a, r, sending):
        ref = (dq_ref, dk_ref, dv_ref)[a]
        at = place if sending else order[r]
        return copy(out_send.at[a, order[r]], ref.at[:, part(at)], out_ssem.at[a, r], out_rsem.at[a, r], base + order[r])

    def start_hop(hop, b):
        for c in hop_copies(hop, b):
            c.start()

    def wait_hop(hop, b):
        for c in hop_copies(hop, b):
            c.wait_recv()

    def work(dz, b, c0, c1, causal, write_dq):
        n = (c1 - c0) * tok
        rows = slice(c0 * tok, c1 * tok)
        live = key_seg[rows, :] == stat[dz, b, 8:9, :]
        if causal:
            key_pos = lax.broadcasted_iota(jnp.int32, (n, tok), 0) + c0 * tok
            query_pos = lax.broadcasted_iota(jnp.int32, (n, tok), 1) + b * tok
            live = live & (key_pos <= query_pos)
        bias = jnp.where(live, 0.0, -1e30)

        def head(h, carry):
            here = pl.ds(pl.multiple_of(h * HEAD_DIM, HEAD_DIM), HEAD_DIM)
            qb, gb = visit[dz, b, 0, :, here], visit[dz, b, 1, :, here]
            kk, vv = keys[rows, here], values[rows, here]
            scores = dot(kk, qb, 1, 1) * (SCALE * LOG2E) - stat[dz, b, pl.ds(h + heads, 1), :]
            prob = jnp.exp2(scores + bias)
            prob_grad = dot(vv, gb, 1, 1)
            score_low = (prob * (prob_grad - stat[dz, b, pl.ds(h, 1), :])).astype(jnp.bfloat16)
            dv_acc[rows, here] += dot(prob.astype(jnp.bfloat16), gb, 1, 0)
            dk_acc[rows, here] += dot(score_low, qb, 1, 0)
            write_dq(here, dot(score_low, kk, 0, 0))
            return carry

        lax.fori_loop(0, heads, head, 0)

    for a in (0, 1, 2):
        for r in (2, 3, 1):
            in_copy(a, r, True).start()

    @pl.when(prev1)
    def _():
        start_hop(0, place)

    for a in (3, 4):
        for r in (2, 3, 1):
            in_copy(a, r, True).start()

    for r in range(1, GROUP):
        for a in (0, 1, 2):
            in_copy(a, r, False).wait_recv()

        @pl.when(prev1)
        def _(r=r):
            start_hop(0, order[r])

    for b in range(GROUP):
        seg = jnp.broadcast_to(stat[0, b, 8:9, :], (tok, tok))
        key_seg[b * tok : (b + 1) * tok, :] = seg.T
    for r in range(1, GROUP):
        for a in (3, 4):
            in_copy(a, r, False).wait_recv()

    for b in range(GROUP):

        def own(here, value, b=b):
            dq_acc[b, :, here] = value

        work(0, b, 0, b + 1, True, own)

    for r in range(GROUP):
        b = order[r]

        @pl.when(next1)
        def _(b=b):
            wait_hop(0, b)

            @pl.when(prev1 & (b < GROUP - 1))
            def _():
                start_hop(1, b)

            def visiting(here, value):
                dq_send[0, b, :, here] = value.astype(jnp.bfloat16)

            work(1, b, 0, GROUP, False, visiting)
            dq_copy(0, b).start()

    for b in range(GROUP - 1):

        @pl.when(next2)
        def _(b=b):
            wait_hop(1, b)

            def visiting(here, value):
                dq_send[1, b, :, here] = value.astype(jnp.bfloat16)

            work(2, b, b + 1, GROUP, False, visiting)
            dq_copy(1, b).start()

    def finish(a, acc, ref, r):
        if r == 0:
            ref[:, part(place)] = acc.astype(jnp.bfloat16)
        else:
            out_send[a, order[r]] = acc.astype(jnp.bfloat16)
            out_copy(a, r, True).start()

    for r in (2, 3, 1, 0):
        finish(1, dk_acc[rows_of(order[r]), :] * SCALE, dk_ref, r)
        finish(2, dv_acc[rows_of(order[r]), :], dv_ref, r)

    for r in (2, 3, 1, 0):
        b = order[r]

        @pl.when(prev1)
        def _(b=b):
            dq_copy(0, b).wait_recv()
            dq_acc[b] += dq_recv[0, b].astype(jnp.float32)

        @pl.when(prev2 & (b < GROUP - 1))
        def _(b=b):
            dq_copy(1, b).wait_recv()
            dq_acc[b] += dq_recv[1, b].astype(jnp.float32)

        finish(0, dq_acc[b] * SCALE, dq_ref, r)

    for r in range(1, GROUP):
        for a in range(5):
            in_copy(a, r, True).wait_send()
        for a in range(3):
            out_copy(a, r, True).wait_send()
            out_copy(a, r, False).wait_recv()

    for b in range(GROUP):

        @pl.when(prev1)
        def _(b=b):
            for c in hop_copies(0, b):
                c.wait_send()

        @pl.when(next1)
        def _(b=b):
            dq_copy(0, b).wait_send()

    for b in range(GROUP - 1):

        @pl.when(prev1 & next1)
        def _(b=b):
            for c in hop_copies(1, b):
                c.wait_send()

        @pl.when(next2)
        def _(b=b):
            dq_copy(1, b).wait_send()


def on_device(queries, key_rows, value_rows, attn_out, out_grad, log_norm, segments):
    tok, width = queries.shape
    cols = width // GROUP
    chain_len = lax.axis_size("ctx")
    bf16, f32 = jnp.bfloat16, jnp.float32
    dma = pltpu.SemaphoreType.DMA
    vmem = pl.BlockSpec(memory_space=pltpu.VMEM)
    return pl.pallas_call(
        functools.partial(kernel, chain_len),
        out_shape=[jax.ShapeDtypeStruct((tok, width), bf16)] * 3,
        in_specs=[vmem] * 7,
        out_specs=[vmem] * 3,
        scratch_shapes=[
            pltpu.VMEM((GROUP, 16, tok), f32),
            pltpu.VMEM((3, GROUP, 2, tok, cols), bf16),
            pltpu.VMEM((3, GROUP, 16, tok), f32),
            pltpu.VMEM((GROUP * tok, cols), bf16),
            pltpu.VMEM((GROUP * tok, cols), bf16),
            pltpu.VMEM((GROUP * tok, tok), f32),
            pltpu.VMEM((GROUP * tok, cols), f32),
            pltpu.VMEM((GROUP * tok, cols), f32),
            pltpu.VMEM((GROUP, tok, cols), f32),
            pltpu.VMEM((2, GROUP, tok, cols), bf16),
            pltpu.VMEM((2, GROUP, tok, cols), bf16),
            pltpu.VMEM((3, GROUP, tok, cols), bf16),
            dma((5, GROUP)), dma((5, GROUP)),
            dma((2, 2, GROUP)), dma((2, 2, GROUP)),
            dma((2, GROUP)), dma((2, GROUP)),
            dma((3, GROUP)), dma((3, GROUP)),
        ],
        compiler_params=pltpu.CompilerParams(
            collective_id=0, has_side_effects=True, vmem_limit_bytes=40 * 1024 * 1024
        ),
        name="attention_backward",
    )(queries, key_rows, value_rows, attn_out, out_grad, log_norm, segments.reshape(1, tok))


def solution(mesh):
    placed = (P(("dp", "ctx"), None),) * 6 + (P(("dp", "ctx")),)
    return jax.shard_map(
        on_device,
        mesh=mesh,
        in_specs=placed,
        out_specs=(P(("dp", "ctx"), None),) * 3,
        check_vma=False,
    )
```

```python
import functools

import jax
import jax.numpy as jnp
from jax import lax
from jax.experimental import pallas as pl
from jax.experimental.pallas import tpu as pltpu
from jax.sharding import PartitionSpec as P

HEAD_DIM = 128
SEQ_DEVS = 8
GROUP = 4
STAGES = 4
LOG2E = 1.4426950408889634
MESH = pl.DeviceIdType.MESH
SCALE = HEAD_DIM ** (-0.5)


def dot(a, b, a_dim, b_dim):
    return lax.dot_general(a, b, (((a_dim,), (b_dim,)), ((), ())), preferred_element_type=jnp.float32)


def kernel(
    chain_len,
    q_ref, k_ref, v_ref, o_ref, g_ref, ln_ref, seg_ref,
    dq_ref, dk_ref, dv_ref,
    o_all, g_all,
    stat_send, visit, stat, keys, values, key_seg, dk_acc, dv_acc, dq_acc,
    dq_send, dq_recv, out_send,
    own_sem, stat_ssem, stat_rsem, in_ssem, in_rsem, hop_ssem, hop_rsem, dq_ssem, dq_rsem, out_ssem, out_rsem,
):
    tok = q_ref.shape[0]
    cols = q_ref.shape[1] // GROUP
    heads = cols // HEAD_DIM
    stages, wide = visit.shape[1], visit.shape[5]
    stage_heads = wide // HEAD_DIM
    me = lax.axis_index("ctx")
    layer = me // GROUP
    place = me % GROUP
    layers = chain_len // GROUP
    base = layer * GROUP
    step = 1 - 2 * (place % 2)

    def nth(r):
        return (place + (r % 2) * step + 2 * (r // 2)) % GROUP

    prev1, prev2 = layer >= 1, layer >= 2
    next1, next2 = layer <= layers - 2, layer <= layers - 3

    def part(p, s):
        return pl.ds(pl.multiple_of(p * cols + s * wide, wide), wide)

    def rows_of(b):
        return pl.ds(pl.multiple_of(b * tok, tok), tok)

    def copy(src, dst, ssem, rsem, to):
        return pltpu.make_async_remote_copy(
            src_ref=src, dst_ref=dst, send_sem=ssem, recv_sem=rsem,
            device_id={"ctx": to}, device_id_type=MESH,
        )

    barrier = pltpu.get_barrier_semaphore()

    def greet(to):
        pl.semaphore_signal(barrier, inc=1, device_id={"ctx": to}, device_id_type=MESH)

    for r in range(1, GROUP):
        greet(base + nth(r))
    for there, to in ((prev1, me - GROUP), (prev2, me - 2 * GROUP), (next1, me + GROUP), (next2, me + 2 * GROUP)):
        pl.when(there)(functools.partial(greet, to))

    def in_ends(a, p, s, at):
        src = (q_ref, g_ref, k_ref, v_ref)[a].at[:, part(p, s)]
        dst = (visit.at[0, s, at, 0], visit.at[0, s, at, 1], keys.at[s, rows_of(at)], values.at[s, rows_of(at)])[a]
        return src, dst

    def own_copy(a, s):
        src, dst = in_ends(a, place, s, place)
        return pltpu.make_async_copy(src, dst, own_sem.at[a, s])

    def in_copy(a, r, s, sending):
        p = nth(r)
        src, dst = in_ends(a, p, s, place if sending else p)
        return copy(src, dst, in_ssem.at[a, r, s], in_rsem.at[a, r, s], base + p)

    def stat_copy(r, sending):
        p = nth(r)
        at = place if sending else p
        return copy(stat_send.at[p], stat.at[0, at], stat_ssem.at[0, r], stat_rsem.at[0, r], base + p)

    def stat_hop(hop, b):
        return copy(stat.at[hop, b], stat.at[hop + 1, b], stat_ssem.at[hop + 1, b], stat_rsem.at[hop + 1, b], me - GROUP)

    def hop_copy(hop, b, s):
        return copy(
            visit.at[hop, s, b], visit.at[hop + 1, s, b], hop_ssem.at[hop, b, s], hop_rsem.at[hop, b, s], me - GROUP
        )

    def dq_copy(d, b, s):
        return copy(
            dq_send.at[d, s, b], dq_recv.at[d, s, b], dq_ssem.at[d, b, s], dq_rsem.at[d, b, s], me + (d + 1) * GROUP
        )

    def out_copy(a, r, s, sending):
        ref = (dq_ref, dk_ref, dv_ref)[a]
        p = nth(r)
        at = place if sending else p
        return copy(
            out_send.at[a, s, p], ref.at[:, part(at, s)], out_ssem.at[a, r, s], out_rsem.at[a, r, s], base + p
        )

    o_copy = pltpu.make_async_copy(o_ref, o_all, own_sem.at[4, 0])
    g_copy = pltpu.make_async_copy(g_ref, g_all, own_sem.at[4, 1])
    o_copy.start()
    g_copy.start()
    for s in range(stages):
        for a in range(4):
            own_copy(a, s).start()
    partners = 3 + prev1.astype(jnp.int32) + prev2.astype(jnp.int32) + next1.astype(jnp.int32) + next2.astype(jnp.int32)
    pl.semaphore_wait(barrier, partners)

    def work(dz, b, c0, c1, s, causal, write_dq):
        n = (c1 - c0) * tok
        rows = slice(c0 * tok, c1 * tok)
        live = key_seg[rows, :] == stat[dz, b, 8:9, :]
        if causal:
            key_pos = lax.broadcasted_iota(jnp.int32, (n, tok), 0) + c0 * tok
            query_pos = lax.broadcasted_iota(jnp.int32, (n, tok), 1) + b * tok
            live = live & (key_pos <= query_pos)
        bias = jnp.where(live, 0.0, -1e30)
        for h in range(stage_heads):
            here = slice(h * HEAD_DIM, (h + 1) * HEAD_DIM)
            row = s * stage_heads + h
            qb, gb = visit[dz, s, b, 0, :, here], visit[dz, s, b, 1, :, here]
            kk, vv = keys[s, rows, here], values[s, rows, here]
            scores = dot(kk, qb, 1, 1) * (SCALE * LOG2E) - stat[dz, b, pl.ds(row + heads, 1), :]
            prob = jnp.exp2(scores + bias)
            prob_grad = dot(vv, gb, 1, 1)
            score_low = (prob * (prob_grad - stat[dz, b, pl.ds(row, 1), :])).astype(jnp.bfloat16)
            dv_add = dot(prob.astype(jnp.bfloat16), gb, 1, 0)
            dk_add = dot(score_low, qb, 1, 0)
            dv_acc[s, rows, here] += dv_add
            dk_acc[s, rows, here] += dk_add
            write_dq(here, dot(score_low, kk, 0, 0))

    def start_in(arrays, s):
        for r in (2, 3, 1):
            for a in arrays:
                in_copy(a, r, s, True).start()

    def finish(a, acc, ref, r, s):
        if r == 0:
            ref[:, part(place, s)] = acc.astype(jnp.bfloat16)
        else:
            out_send[a, s, nth(r)] = acc.astype(jnp.bfloat16)
            out_copy(a, r, s, True).start()

    def own_hop(s):
        for a in (0, 1):
            own_copy(a, s).wait()

        @pl.when(prev1)
        def _():
            hop_copy(0, place, s).start()

    def own_stage(s):
        for r in range(1, GROUP):
            for a in (0, 1):
                in_copy(a, r, s, False).wait_recv()

            @pl.when(prev1)
            def _(r=r):
                hop_copy(0, nth(r), s).start()

    def own_work(s):
        for a in (2, 3):
            own_copy(a, s).wait()
            for r in range(1, GROUP):
                in_copy(a, r, s, False).wait_recv()
        dk_acc[s] = jnp.zeros(dk_acc.shape[1:], jnp.float32)
        dv_acc[s] = jnp.zeros(dv_acc.shape[1:], jnp.float32)
        for b in range(GROUP):

            def own(here, value, b=b):
                dq_acc[s, b, :, here] = value

            work(0, b, 0, b + 1, s, True, own)

    def forward(s):
        for r in range(GROUP):
            b = nth(r)
            hop_copy(0, b, s).wait_recv()

            @pl.when(prev1 & (b < GROUP - 1))
            def _(b=b):
                hop_copy(1, b, s).start()

    def stat_arrived():
        for r in range(GROUP):
            b = nth(r)
            stat_hop(0, b).wait_recv()

            @pl.when(prev1 & (b < GROUP - 1))
            def _(b=b):
                stat_hop(1, b).start()

    def next_work(s):
        def one(r, carry):
            b = nth(r)

            def visiting(here, value):
                dq_send[0, s, b, :, here] = value.astype(jnp.bfloat16)

            work(1, b, 0, GROUP, s, False, visiting)
            dq_copy(0, b, s).start()
            return carry

        lax.fori_loop(0, GROUP, one, 0)

    def last_work(s):
        for b in range(GROUP - 1):

            @pl.when(s == 0)
            def _(b=b):
                stat_hop(1, b).wait_recv()

            hop_copy(1, b, s).wait_recv()

            def visiting(here, value, b=b):
                dq_send[1, s, b, :, here] = value.astype(jnp.bfloat16)

            work(2, b, b + 1, GROUP, s, False, visiting)
            dq_copy(1, b, s).start()

    def key_results(s):
        for r in (2, 3, 1, 0):
            finish(1, dk_acc[s, rows_of(nth(r)), :] * SCALE, dk_ref, r, s)
            finish(2, dv_acc[s, rows_of(nth(r)), :], dv_ref, r, s)

    def query_results(s):
        for r in (2, 3, 1, 0):
            b = nth(r)

            @pl.when(prev1)
            def _(b=b):
                dq_copy(0, b, s).wait_recv()
                dq_acc[s, b] += dq_recv[0, s, b].astype(jnp.float32)

            @pl.when(prev2 & (b < GROUP - 1))
            def _(b=b):
                dq_copy(1, b, s).wait_recv()
                dq_acc[s, b] += dq_recv[1, s, b].astype(jnp.float32)

            finish(0, dq_acc[s, b] * SCALE, dq_ref, r, s)

    start_in((0, 1), 0)
    own_hop(0)
    if stages > 1:
        own_hop(1)
    o_copy.wait()
    g_copy.wait()

    lane = lax.broadcasted_iota(jnp.int32, (tok, 128), 1)
    table = jnp.zeros((tok, 128), jnp.float32)
    for h in range(GROUP * heads):
        here = slice(h * HEAD_DIM, (h + 1) * HEAD_DIM)
        delta = jnp.sum(g_all[:, here].astype(jnp.float32) * o_all[:, here].astype(jnp.float32), axis=1, keepdims=True)
        table = jnp.where(lane == (h // heads) * 8 + h % heads, delta, table)
    table = table.T
    seg_rows = jnp.broadcast_to(seg_ref[...].astype(jnp.float32), (8, tok))
    for p in range(GROUP):
        stat_send[p, 0:heads, :] = table[8 * p : 8 * p + heads, :]
        stat_send[p, heads : 2 * heads, :] = ln_ref[p * heads : (p + 1) * heads, :] * LOG2E
        stat_send[p, 8:16, :] = seg_rows
    stat[0, place] = stat_send[place]

    for r in (2, 3, 1):
        stat_copy(r, True).start()
    own_stage(0)
    if stages > 1:
        start_in((0, 1), 1)
    start_in((2, 3), 0)
    for r in range(GROUP):
        if r:
            stat_copy(r, False).wait_recv()

        @pl.when(prev1)
        def _(r=r):
            stat_hop(0, nth(r)).start()

    for b in range(GROUP):
        seg = jnp.broadcast_to(stat[0, b, 8:9, :], (tok, tok))
        key_seg[b * tok : (b + 1) * tok, :] = seg.T

    def turn(i, carry):
        @pl.when(i + 1 < stages)
        def _():
            own_stage(i + 1)

        @pl.when(i + 2 < stages)
        def _():
            start_in((0, 1), i + 2)
            own_hop(i + 2)

        @pl.when((i < stages) & next1)
        def _():
            pl.when(i == 0)(stat_arrived)
            forward(i)

        @pl.when(i < stages)
        def _():
            own_work(i)

        @pl.when(i + 1 < stages)
        def _():
            start_in((2, 3), i + 1)

        @pl.when((i < stages) & next1)
        def _():
            next_work(i)

        @pl.when((i >= 1) & (i <= stages))
        def _():
            pl.when(next2)(functools.partial(last_work, i - 1))
            key_results(i - 1)

        @pl.when(i >= 2)
        def _():
            query_results(i - 2)

        return carry

    lax.fori_loop(0, stages + 2, turn, 0)

    for r in range(1, GROUP):
        stat_copy(r, True).wait_send()
    for b in range(GROUP):
        pl.when(prev1)(stat_hop(0, b).wait_send)
        if b < GROUP - 1:
            pl.when(prev1 & next1)(stat_hop(1, b).wait_send)

    def drain(s, carry):
        for r in range(1, GROUP):
            for a in range(4):
                in_copy(a, r, s, True).wait_send()
            for a in range(3):
                out_copy(a, r, s, True).wait_send()
                out_copy(a, r, s, False).wait_recv()
        for b in range(GROUP):
            pl.when(prev1)(hop_copy(0, b, s).wait_send)
            pl.when(next1)(dq_copy(0, b, s).wait_send)
            if b < GROUP - 1:
                pl.when(prev1 & next1)(hop_copy(1, b, s).wait_send)
                pl.when(next2)(dq_copy(1, b, s).wait_send)
        return carry

    lax.fori_loop(0, stages, drain, 0)


def on_device(queries, key_rows, value_rows, attn_out, out_grad, log_norm, segments):
    tok, width = queries.shape
    cols = width // GROUP
    stages = STAGES
    wide = cols // stages
    chain_len = lax.axis_size("ctx")
    bf16, f32 = jnp.bfloat16, jnp.float32
    dma = pltpu.SemaphoreType.DMA
    vmem = pl.BlockSpec(memory_space=pltpu.VMEM)
    far = pl.BlockSpec(memory_space=pl.ANY)
    return pl.pallas_call(
        functools.partial(kernel, chain_len),
        out_shape=[jax.ShapeDtypeStruct((tok, width), bf16)] * 3,
        in_specs=[far] * 5 + [vmem] * 2,
        out_specs=[vmem] * 3,
        scratch_shapes=[
            pltpu.VMEM((tok, width), bf16),
            pltpu.VMEM((tok, width), bf16),
            pltpu.VMEM((GROUP, 16, tok), f32),
            pltpu.VMEM((3, stages, GROUP, 2, tok, wide), bf16),
            pltpu.VMEM((3, GROUP, 16, tok), f32),
            pltpu.VMEM((stages, GROUP * tok, wide), bf16),
            pltpu.VMEM((stages, GROUP * tok, wide), bf16),
            pltpu.VMEM((GROUP * tok, tok), f32),
            pltpu.VMEM((stages, GROUP * tok, wide), f32),
            pltpu.VMEM((stages, GROUP * tok, wide), f32),
            pltpu.VMEM((stages, GROUP, tok, wide), f32),
            pltpu.VMEM((2, stages, GROUP, tok, wide), bf16),
            pltpu.VMEM((2, stages, GROUP, tok, wide), bf16),
            pltpu.VMEM((3, stages, GROUP, tok, wide), bf16),
            dma((5, max(stages, 2))),
            dma((3, GROUP)), dma((3, GROUP)),
            dma((4, GROUP, stages)), dma((4, GROUP, stages)),
            dma((2, GROUP, stages)), dma((2, GROUP, stages)),
            dma((2, GROUP, stages)), dma((2, GROUP, stages)),
            dma((3, GROUP, stages)), dma((3, GROUP, stages)),
        ],
        compiler_params=pltpu.CompilerParams(
            collective_id=0, has_side_effects=True, vmem_limit_bytes=40 * 1024 * 1024
        ),
        name="attention_backward",
    )(queries, key_rows, value_rows, attn_out, out_grad, log_norm.T, segments.reshape(1, tok))


def solution(mesh):
    placed = (P(("dp", "ctx"), None),) * 6 + (P(("dp", "ctx")),)
    return jax.shard_map(
        on_device,
        mesh=mesh,
        in_specs=placed,
        out_specs=(P(("dp", "ctx"), None),) * 3,
        check_vma=False,
    )
```

```python
import functools

import jax
import jax.numpy as jnp
from jax import lax
from jax.experimental import pallas as pl
from jax.experimental.pallas import tpu as pltpu
from jax.sharding import PartitionSpec as P

HEAD_DIM = 128
SEQ_DEVS = 8
GROUP = 4
STAGES = 4
LOG2E = 1.4426950408889634
MESH = pl.DeviceIdType.MESH
SCALE = HEAD_DIM ** (-0.5)


def dot(a, b, a_dim, b_dim):
    return lax.dot_general(a, b, (((a_dim,), (b_dim,)), ((), ())), preferred_element_type=jnp.float32)


def kernel(
    chain_len,
    q_ref, k_ref, v_ref, o_ref, g_ref, ln_far, seg_far,
    dq_ref, dk_ref, dv_ref,
    o_all, g_all, ln_ref, seg_ref,
    stat_send, visit, stat, keys, values, key_seg, dk_acc, dv_acc, dq_acc,
    dq_send, dq_recv, out_send,
    own_sem, stat_ssem, stat_rsem, in_ssem, in_rsem, hop_ssem, hop_rsem, dq_ssem, dq_rsem, out_ssem, out_rsem,
):
    tok = q_ref.shape[0]
    cols = q_ref.shape[1] // GROUP
    heads = cols // HEAD_DIM
    stages, wide = visit.shape[1], visit.shape[5]
    stage_heads = wide // HEAD_DIM
    me = lax.axis_index("ctx")
    layer = me // GROUP
    place = me % GROUP
    layers = chain_len // GROUP
    base = layer * GROUP
    step = 1 - 2 * (place % 2)

    def nth(r):
        return (place + (r % 2) * step + 2 * (r // 2)) % GROUP

    prev1, prev2 = layer >= 1, layer >= 2
    next1, next2 = layer <= layers - 2, layer <= layers - 3

    def part(p, s):
        return pl.ds(pl.multiple_of(p * cols + s * wide, wide), wide)

    def rows_of(b):
        return pl.ds(pl.multiple_of(b * tok, tok), tok)

    def copy(src, dst, ssem, rsem, to):
        return pltpu.make_async_remote_copy(
            src_ref=src, dst_ref=dst, send_sem=ssem, recv_sem=rsem,
            device_id={"ctx": to}, device_id_type=MESH,
        )

    barrier = pltpu.get_barrier_semaphore()

    def greet(to):
        pl.semaphore_signal(barrier, inc=1, device_id={"ctx": to}, device_id_type=MESH)

    for r in range(1, GROUP):
        greet(base + nth(r))
    for there, to in ((prev1, me - GROUP), (prev2, me - 2 * GROUP), (next1, me + GROUP), (next2, me + 2 * GROUP)):
        pl.when(there)(functools.partial(greet, to))

    def in_ends(a, p, s, at):
        src = (q_ref, g_ref, k_ref, v_ref)[a].at[:, part(p, s)]
        dst = (visit.at[0, s, at, 0], visit.at[0, s, at, 1], keys.at[s, rows_of(at)], values.at[s, rows_of(at)])[a]
        return src, dst

    def own_copy(a, s):
        src, dst = in_ends(a, place, s, place)
        return pltpu.make_async_copy(src, dst, own_sem.at[a, s])

    def in_copy(a, r, s, sending):
        p = nth(r)
        src, dst = in_ends(a, p, s, place if sending else p)
        return copy(src, dst, in_ssem.at[a, r, s], in_rsem.at[a, r, s], base + p)

    def stat_copy(r, sending):
        p = nth(r)
        at = place if sending else p
        return copy(stat_send.at[p], stat.at[0, at], stat_ssem.at[0, r], stat_rsem.at[0, r], base + p)

    def stat_hop(hop, b):
        return copy(stat.at[hop, b], stat.at[hop + 1, b], stat_ssem.at[hop + 1, b], stat_rsem.at[hop + 1, b], me - GROUP)

    def hop_copy(hop, b, s):
        return copy(
            visit.at[hop, s, b], visit.at[hop + 1, s, b], hop_ssem.at[hop, b, s], hop_rsem.at[hop, b, s], me - GROUP
        )

    def dq_copy(d, b, s):
        return copy(
            dq_send.at[d, s, b], dq_recv.at[d, s, b], dq_ssem.at[d, b, s], dq_rsem.at[d, b, s], me + (d + 1) * GROUP
        )

    def out_copy(a, r, s, sending):
        ref = (dq_ref, dk_ref, dv_ref)[a]
        p = nth(r)
        at = place if sending else p
        return copy(
            out_send.at[a, s, p], ref.at[:, part(at, s)], out_ssem.at[a, r, s], out_rsem.at[a, r, s], base + p
        )

    o_copy = pltpu.make_async_copy(o_ref, o_all, own_sem.at[4, 0])
    g_copy = pltpu.make_async_copy(g_ref, g_all, own_sem.at[4, 1])
    ln_copy = pltpu.make_async_copy(ln_far, ln_ref, own_sem.at[4, 2])
    seg_copy = pltpu.make_async_copy(seg_far, seg_ref, own_sem.at[4, 3])
    for c in (o_copy, g_copy, ln_copy, seg_copy):
        c.start()
    for a in range(4):
        for s in range(stages):
            own_copy(a, s).start()
    partners = 3 + prev1.astype(jnp.int32) + prev2.astype(jnp.int32) + next1.astype(jnp.int32) + next2.astype(jnp.int32)
    pl.semaphore_wait(barrier, partners)

    def work(dz, b, c0, c1, s, causal, write_dq):
        n = (c1 - c0) * tok
        rows = slice(c0 * tok, c1 * tok)
        live = key_seg[rows, :] == stat[dz, b, 8:9, :]
        if causal:
            key_pos = lax.broadcasted_iota(jnp.int32, (n, tok), 0) + c0 * tok
            query_pos = lax.broadcasted_iota(jnp.int32, (n, tok), 1) + b * tok
            live = live & (key_pos <= query_pos)
        bias = jnp.where(live, 0.0, -1e30)
        for h in range(stage_heads):
            here = slice(h * HEAD_DIM, (h + 1) * HEAD_DIM)
            row = s * stage_heads + h
            qb, gb = visit[dz, s, b, 0, :, here], visit[dz, s, b, 1, :, here]
            kk, vv = keys[s, rows, here], values[s, rows, here]
            scores = dot(kk, qb, 1, 1) * (SCALE * LOG2E) - stat[dz, b, pl.ds(row + heads, 1), :]
            prob = jnp.exp2(scores + bias)
            prob_grad = dot(vv, gb, 1, 1)
            score_low = (prob * (prob_grad - stat[dz, b, pl.ds(row, 1), :])).astype(jnp.bfloat16)
            dv_add = dot(prob.astype(jnp.bfloat16), gb, 1, 0)
            dk_add = dot(score_low, qb, 1, 0)
            dv_acc[s, rows, here] += dv_add
            dk_acc[s, rows, here] += dk_add
            write_dq(here, dot(score_low, kk, 0, 0))

    def start_in(arrays, s):
        for r in (2, 3, 1):
            for a in arrays:
                in_copy(a, r, s, True).start()

    def finish(a, acc, ref, r, s):
        if r == 0:
            ref[:, part(place, s)] = acc.astype(jnp.bfloat16)
        else:
            out_send[a, s, nth(r)] = acc.astype(jnp.bfloat16)
            out_copy(a, r, s, True).start()

    def own_hop(s):
        for a in (0, 1):
            own_copy(a, s).wait()

        @pl.when(prev1)
        def _():
            hop_copy(0, place, s).start()

    def own_stage(s):
        for r in range(1, GROUP):
            for a in (0, 1):
                in_copy(a, r, s, False).wait_recv()

            @pl.when(prev1)
            def _(r=r):
                hop_copy(0, nth(r), s).start()

    def own_work(s):
        for a in (2, 3):
            own_copy(a, s).wait()
            for r in range(1, GROUP):
                in_copy(a, r, s, False).wait_recv()
        dk_acc[s] = jnp.zeros(dk_acc.shape[1:], jnp.float32)
        dv_acc[s] = jnp.zeros(dv_acc.shape[1:], jnp.float32)
        for b in range(GROUP):

            def own(here, value, b=b):
                dq_acc[s, b, :, here] = value

            work(0, b, 0, b + 1, s, True, own)

    def forward(s):
        for r in range(GROUP):
            b = nth(r)
            hop_copy(0, b, s).wait_recv()

            @pl.when(prev1 & (b < GROUP - 1))
            def _(b=b):
                hop_copy(1, b, s).start()

    def stat_arrived():
        for r in range(GROUP):
            b = nth(r)
            stat_hop(0, b).wait_recv()

            @pl.when(prev1 & (b < GROUP - 1))
            def _(b=b):
                stat_hop(1, b).start()

    def next_work(s):
        def one(r, carry):
            b = nth(r)

            def visiting(here, value):
                dq_send[0, s, b, :, here] = value.astype(jnp.bfloat16)

            work(1, b, 0, GROUP, s, False, visiting)
            dq_copy(0, b, s).start()
            return carry

        lax.fori_loop(0, GROUP, one, 0)

    def last_work(s):
        for b in range(GROUP - 1):

            @pl.when(s == 0)
            def _(b=b):
                stat_hop(1, b).wait_recv()

            hop_copy(1, b, s).wait_recv()

            def visiting(here, value, b=b):
                dq_send[1, s, b, :, here] = value.astype(jnp.bfloat16)

            work(2, b, b + 1, GROUP, s, False, visiting)
            dq_copy(1, b, s).start()

    def key_results(s):
        for r in (2, 3, 1, 0):
            finish(1, dk_acc[s, rows_of(nth(r)), :] * SCALE, dk_ref, r, s)
            finish(2, dv_acc[s, rows_of(nth(r)), :], dv_ref, r, s)

    def query_results(s):
        for r in (2, 3, 1, 0):
            b = nth(r)

            @pl.when(prev1)
            def _(b=b):
                dq_copy(0, b, s).wait_recv()
                dq_acc[s, b] += dq_recv[0, s, b].astype(jnp.float32)

            @pl.when(prev2 & (b < GROUP - 1))
            def _(b=b):
                dq_copy(1, b, s).wait_recv()
                dq_acc[s, b] += dq_recv[1, s, b].astype(jnp.float32)

            finish(0, dq_acc[s, b] * SCALE, dq_ref, r, s)

    start_in((0, 1), 0)
    for s in range(stages):
        own_hop(s)
    o_copy.wait()
    g_copy.wait()
    ln_copy.wait()
    seg_copy.wait()

    lane = lax.broadcasted_iota(jnp.int32, (tok, 128), 1)
    table = jnp.zeros((tok, 128), jnp.float32)
    for h in range(GROUP * heads):
        here = slice(h * HEAD_DIM, (h + 1) * HEAD_DIM)
        delta = jnp.sum(g_all[:, here].astype(jnp.float32) * o_all[:, here].astype(jnp.float32), axis=1, keepdims=True)
        table = jnp.where(lane == (h // heads) * 8 + h % heads, delta, table)
    table = table.T
    seg_rows = jnp.broadcast_to(seg_ref[...].astype(jnp.float32), (8, tok))
    for p in range(GROUP):
        stat_send[p, 0:heads, :] = table[8 * p : 8 * p + heads, :]
        stat_send[p, heads : 2 * heads, :] = ln_ref[p * heads : (p + 1) * heads, :] * LOG2E
        stat_send[p, 8:16, :] = seg_rows
    stat[0, place] = stat_send[place]

    for r in (2, 3, 1):
        stat_copy(r, True).start()
    own_stage(0)
    if stages > 1:
        start_in((0, 1), 1)
    start_in((2, 3), 0)
    for r in range(GROUP):
        if r:
            stat_copy(r, False).wait_recv()

        @pl.when(prev1)
        def _(r=r):
            stat_hop(0, nth(r)).start()

    for b in range(GROUP):
        seg = jnp.broadcast_to(stat[0, b, 8:9, :], (tok, tok))
        key_seg[b * tok : (b + 1) * tok, :] = seg.T

    def turn(i, carry):
        @pl.when(i + 1 < stages)
        def _():
            own_stage(i + 1)

        @pl.when(i + 2 < stages)
        def _():
            start_in((0, 1), i + 2)

        @pl.when((i < stages) & next1)
        def _():
            pl.when(i == 0)(stat_arrived)
            forward(i)

        @pl.when(i < stages)
        def _():
            own_work(i)

        @pl.when(i + 1 < stages)
        def _():
            start_in((2, 3), i + 1)

        @pl.when((i < stages) & next1)
        def _():
            next_work(i)

        @pl.when((i >= 1) & (i <= stages))
        def _():
            pl.when(next2)(functools.partial(last_work, i - 1))
            key_results(i - 1)

        @pl.when(i >= 2)
        def _():
            query_results(i - 2)

        return carry

    lax.fori_loop(0, stages + 2, turn, 0)

    for r in range(1, GROUP):
        stat_copy(r, True).wait_send()
    for b in range(GROUP):
        pl.when(prev1)(stat_hop(0, b).wait_send)
        if b < GROUP - 1:
            pl.when(prev1 & next1)(stat_hop(1, b).wait_send)

    def drain(s, carry):
        for r in range(1, GROUP):
            for a in range(4):
                in_copy(a, r, s, True).wait_send()
            for a in range(3):
                out_copy(a, r, s, True).wait_send()
                out_copy(a, r, s, False).wait_recv()
        for b in range(GROUP):
            pl.when(prev1)(hop_copy(0, b, s).wait_send)
            pl.when(next1)(dq_copy(0, b, s).wait_send)
            if b < GROUP - 1:
                pl.when(prev1 & next1)(hop_copy(1, b, s).wait_send)
                pl.when(next2)(dq_copy(1, b, s).wait_send)
        return carry

    lax.fori_loop(0, stages, drain, 0)


def on_device(queries, key_rows, value_rows, attn_out, out_grad, log_norm, segments):
    tok, width = queries.shape
    cols = width // GROUP
    stages = STAGES
    wide = cols // stages
    chain_len = lax.axis_size("ctx")
    bf16, f32 = jnp.bfloat16, jnp.float32
    dma = pltpu.SemaphoreType.DMA
    vmem = pl.BlockSpec(memory_space=pltpu.VMEM)
    far = pl.BlockSpec(memory_space=pltpu.HBM)
    return pl.pallas_call(
        functools.partial(kernel, chain_len),
        out_shape=[jax.ShapeDtypeStruct((tok, width), bf16)] * 3,
        in_specs=[far] * 7,
        out_specs=[vmem] * 3,
        scratch_shapes=[
            pltpu.VMEM((tok, width), bf16),
            pltpu.VMEM((tok, width), bf16),
            pltpu.VMEM(log_norm.shape[::-1], f32),
            pltpu.VMEM((1, tok), jnp.int32),
            pltpu.VMEM((GROUP, 16, tok), f32),
            pltpu.VMEM((3, stages, GROUP, 2, tok, wide), bf16),
            pltpu.VMEM((3, GROUP, 16, tok), f32),
            pltpu.VMEM((stages, GROUP * tok, wide), bf16),
            pltpu.VMEM((stages, GROUP * tok, wide), bf16),
            pltpu.VMEM((GROUP * tok, tok), f32),
            pltpu.VMEM((stages, GROUP * tok, wide), f32),
            pltpu.VMEM((stages, GROUP * tok, wide), f32),
            pltpu.VMEM((stages, GROUP, tok, wide), f32),
            pltpu.VMEM((2, stages, GROUP, tok, wide), bf16),
            pltpu.VMEM((2, stages, GROUP, tok, wide), bf16),
            pltpu.VMEM((3, stages, GROUP, tok, wide), bf16),
            dma((5, max(stages, 4))),
            dma((3, GROUP)), dma((3, GROUP)),
            dma((4, GROUP, stages)), dma((4, GROUP, stages)),
            dma((2, GROUP, stages)), dma((2, GROUP, stages)),
            dma((2, GROUP, stages)), dma((2, GROUP, stages)),
            dma((3, GROUP, stages)), dma((3, GROUP, stages)),
        ],
        compiler_params=pltpu.CompilerParams(
            collective_id=0, has_side_effects=True, vmem_limit_bytes=62 * 1024 * 1024
        ),
        name="attention_backward",
    )(queries, key_rows, value_rows, attn_out, out_grad, log_norm.T, segments.reshape(1, tok))


def solution(mesh):
    placed = (P(("dp", "ctx"), None),) * 6 + (P(("dp", "ctx")),)
    return jax.shard_map(
        on_device,
        mesh=mesh,
        in_specs=placed,
        out_specs=(P(("dp", "ctx"), None),) * 3,
        check_vma=False,
    )
```

```python
import functools

import jax
import jax.numpy as jnp
from jax import lax
from jax.experimental import pallas as pl
from jax.experimental.pallas import tpu as pltpu
from jax.sharding import PartitionSpec as P

HEAD_DIM = 128
SEQ_DEVS = 8
GROUP = 4
STAGES = 4
LOG2E = 1.4426950408889634
MESH = pl.DeviceIdType.MESH
SCALE = HEAD_DIM ** (-0.5)


def dot(a, b, a_dim, b_dim):
    return lax.dot_general(a, b, (((a_dim,), (b_dim,)), ((), ())), preferred_element_type=jnp.float32)


def kernel(
    chain_len,
    q_ref, k_ref, v_ref, o_ref, g_ref, ln_far, seg_far,
    dq_ref, dk_ref, dv_ref,
    o_all, g_all, ln_ref, seg_ref,
    stat_send, visit, stat, keys, values, key_seg, dk_acc, dv_acc, dq_acc,
    dq_send, dq_recv, out_send,
    own_sem, stat_ssem, stat_rsem, in_ssem, in_rsem, hop_ssem, hop_rsem, dq_ssem, dq_rsem, out_ssem, out_rsem,
):
    tok = q_ref.shape[0]
    cols = q_ref.shape[1] // GROUP
    heads = cols // HEAD_DIM
    stages, wide = visit.shape[1], visit.shape[5]
    stage_heads = wide // HEAD_DIM
    me = lax.axis_index("ctx")
    layer = me // GROUP
    place = me % GROUP
    layers = chain_len // GROUP
    base = layer * GROUP
    step = 1 - 2 * (place % 2)

    def nth(r):
        return (place + (r % 2) * step + 2 * (r // 2)) % GROUP

    prev1, prev2 = layer >= 1, layer >= 2
    next1, next2 = layer <= layers - 2, layer <= layers - 3

    def part(p, s):
        return pl.ds(pl.multiple_of(p * cols + s * wide, wide), wide)

    def rows_of(b):
        return pl.ds(pl.multiple_of(b * tok, tok), tok)

    def copy(src, dst, ssem, rsem, to):
        return pltpu.make_async_remote_copy(
            src_ref=src, dst_ref=dst, send_sem=ssem, recv_sem=rsem,
            device_id={"ctx": to}, device_id_type=MESH,
        )

    barrier = pltpu.get_barrier_semaphore()

    def greet(to):
        pl.semaphore_signal(barrier, inc=1, device_id={"ctx": to}, device_id_type=MESH)

    for r in range(1, GROUP):
        greet(base + nth(r))
    for there, to in ((prev1, me - GROUP), (prev2, me - 2 * GROUP), (next1, me + GROUP), (next2, me + 2 * GROUP)):
        pl.when(there)(functools.partial(greet, to))

    def in_ends(a, p, s, at):
        src = (q_ref, g_ref, k_ref, v_ref)[a].at[:, part(p, s)]
        dst = (visit.at[0, s, at, 0], visit.at[0, s, at, 1], keys.at[s, rows_of(at)], values.at[s, rows_of(at)])[a]
        return src, dst

    def own_copy(a, s):
        src, dst = in_ends(a, place, s, place)
        return pltpu.make_async_copy(src, dst, own_sem.at[a, s])

    def in_copy(a, r, s, sending):
        p = nth(r)
        src, dst = in_ends(a, p, s, place if sending else p)
        return copy(src, dst, in_ssem.at[a, r, s], in_rsem.at[a, r, s], base + p)

    def stat_copy(r, sending):
        p = nth(r)
        at = place if sending else p
        return copy(stat_send.at[p], stat.at[0, at], stat_ssem.at[0, r], stat_rsem.at[0, r], base + p)

    def stat_hop(hop, b):
        return copy(stat.at[hop, b], stat.at[hop + 1, b], stat_ssem.at[hop + 1, b], stat_rsem.at[hop + 1, b], me - GROUP)

    def hop_copy(hop, b, s):
        return copy(
            visit.at[hop, s, b], visit.at[hop + 1, s, b], hop_ssem.at[hop, b, s], hop_rsem.at[hop, b, s], me - GROUP
        )

    def dq_copy(d, b, s):
        return copy(
            dq_send.at[d, s, b], dq_recv.at[d, s, b], dq_ssem.at[d, b, s], dq_rsem.at[d, b, s], me + (d + 1) * GROUP
        )

    def out_copy(a, r, s, sending):
        ref = (dq_ref, dk_ref, dv_ref)[a]
        p = nth(r)
        at = place if sending else p
        return copy(
            out_send.at[a, s, p], ref.at[:, part(at, s)], out_ssem.at[a, r, s], out_rsem.at[a, r, s], base + p
        )

    o_copy = pltpu.make_async_copy(o_ref, o_all, own_sem.at[4, 0])
    g_copy = pltpu.make_async_copy(g_ref, g_all, own_sem.at[4, 1])
    ln_copy = pltpu.make_async_copy(ln_far, ln_ref, own_sem.at[4, 2])
    seg_copy = pltpu.make_async_copy(seg_far, seg_ref, own_sem.at[4, 3])
    for c in (o_copy, g_copy, ln_copy, seg_copy):
        c.start()
    for a in range(4):
        for s in range(stages):
            own_copy(a, s).start()
    partners = 3 + prev1.astype(jnp.int32) + prev2.astype(jnp.int32) + next1.astype(jnp.int32) + next2.astype(jnp.int32)
    pl.semaphore_wait(barrier, partners)

    def work(dz, b, c0, c1, s, causal, write_dq):
        n = (c1 - c0) * tok
        rows = slice(c0 * tok, c1 * tok)
        live = key_seg[rows, :] == stat[dz, b, 8:9, :]
        if causal:
            key_pos = lax.broadcasted_iota(jnp.int32, (n, tok), 0) + c0 * tok
            query_pos = lax.broadcasted_iota(jnp.int32, (n, tok), 1) + b * tok
            live = live & (key_pos <= query_pos)
        bias = jnp.where(live, 0.0, -1e30)
        for h in range(stage_heads):
            here = slice(h * HEAD_DIM, (h + 1) * HEAD_DIM)
            row = s * stage_heads + h
            qb, gb = visit[dz, s, b, 0, :, here], visit[dz, s, b, 1, :, here]
            kk, vv = keys[s, rows, here], values[s, rows, here]
            scores = dot(kk, qb, 1, 1) * (SCALE * LOG2E) - stat[dz, b, pl.ds(row + heads, 1), :]
            prob = jnp.exp2(scores + bias)
            prob_grad = dot(vv, gb, 1, 1)
            score_low = (prob * (prob_grad - stat[dz, b, pl.ds(row, 1), :])).astype(jnp.bfloat16)
            dv_add = dot(prob.astype(jnp.bfloat16), gb, 1, 0)
            dk_add = dot(score_low, qb, 1, 0)
            dv_acc[s, rows, here] += dv_add
            dk_acc[s, rows, here] += dk_add
            write_dq(here, dot(score_low, kk, 0, 0))

    def start_in(arrays, s):
        for r in (2, 3, 1):
            for a in arrays:
                in_copy(a, r, s, True).start()

    def out_own(a, s):
        ref = (dq_ref, dk_ref, dv_ref)[a]
        return pltpu.make_async_copy(out_send.at[a, s, place], ref.at[:, part(place, s)], out_ssem.at[a, 0, s])

    def finish(a, acc, ref, r, s):
        out_send[a, s, nth(r)] = acc.astype(jnp.bfloat16)
        if r == 0:
            out_own(a, s).start()
        else:
            out_copy(a, r, s, True).start()

    def own_hop(s):
        for a in (0, 1):
            own_copy(a, s).wait()

        @pl.when(prev1)
        def _():
            hop_copy(0, place, s).start()

    def own_stage(s):
        for r in range(1, GROUP):
            for a in (0, 1):
                in_copy(a, r, s, False).wait_recv()

            @pl.when(prev1)
            def _(r=r):
                hop_copy(0, nth(r), s).start()

    def own_work(s):
        for a in (2, 3):
            own_copy(a, s).wait()
            for r in range(1, GROUP):
                in_copy(a, r, s, False).wait_recv()
        dk_acc[s] = jnp.zeros(dk_acc.shape[1:], jnp.float32)
        dv_acc[s] = jnp.zeros(dv_acc.shape[1:], jnp.float32)
        for b in range(GROUP):

            def own(here, value, b=b):
                dq_acc[s, b, :, here] = value

            work(0, b, 0, b + 1, s, True, own)

    def forward(s):
        for r in range(GROUP):
            b = nth(r)
            hop_copy(0, b, s).wait_recv()

            @pl.when(prev1 & (b < GROUP - 1))
            def _(b=b):
                hop_copy(1, b, s).start()

    def stat_arrived():
        for r in range(GROUP):
            b = nth(r)
            stat_hop(0, b).wait_recv()

            @pl.when(prev1 & (b < GROUP - 1))
            def _(b=b):
                stat_hop(1, b).start()

    def next_work(s):
        def one(r, carry):
            b = nth(r)

            def visiting(here, value):
                dq_send[0, s, b, :, here] = value.astype(jnp.bfloat16)

            work(1, b, 0, GROUP, s, False, visiting)
            dq_copy(0, b, s).start()
            return carry

        lax.fori_loop(0, GROUP, one, 0)

    def last_work(s):
        for b in range(GROUP - 1):

            @pl.when(s == 0)
            def _(b=b):
                stat_hop(1, b).wait_recv()

            hop_copy(1, b, s).wait_recv()

            def visiting(here, value, b=b):
                dq_send[1, s, b, :, here] = value.astype(jnp.bfloat16)

            work(2, b, b + 1, GROUP, s, False, visiting)
            dq_copy(1, b, s).start()

    def key_results(s):
        for r in (2, 3, 1, 0):
            finish(1, dk_acc[s, rows_of(nth(r)), :] * SCALE, dk_ref, r, s)
            finish(2, dv_acc[s, rows_of(nth(r)), :], dv_ref, r, s)

    def query_results(s):
        for r in (2, 3, 1, 0):
            b = nth(r)

            @pl.when(prev1)
            def _(b=b):
                dq_copy(0, b, s).wait_recv()
                dq_acc[s, b] += dq_recv[0, s, b].astype(jnp.float32)

            @pl.when(prev2 & (b < GROUP - 1))
            def _(b=b):
                dq_copy(1, b, s).wait_recv()
                dq_acc[s, b] += dq_recv[1, s, b].astype(jnp.float32)

            finish(0, dq_acc[s, b] * SCALE, dq_ref, r, s)

    start_in((0, 1), 0)
    for s in range(stages):
        own_hop(s)
    o_copy.wait()
    g_copy.wait()
    ln_copy.wait()
    seg_copy.wait()

    lane = lax.broadcasted_iota(jnp.int32, (tok, 128), 1)
    table = jnp.zeros((tok, 128), jnp.float32)
    for h in range(GROUP * heads):
        here = slice(h * HEAD_DIM, (h + 1) * HEAD_DIM)
        delta = jnp.sum(g_all[:, here].astype(jnp.float32) * o_all[:, here].astype(jnp.float32), axis=1, keepdims=True)
        table = jnp.where(lane == (h // heads) * 8 + h % heads, delta, table)
    table = table.T
    seg_rows = jnp.broadcast_to(seg_ref[...].astype(jnp.float32), (8, tok))
    for p in range(GROUP):
        stat_send[p, 0:heads, :] = table[8 * p : 8 * p + heads, :]
        stat_send[p, heads : 2 * heads, :] = ln_ref[p * heads : (p + 1) * heads, :] * LOG2E
        stat_send[p, 8:16, :] = seg_rows
    stat[0, place] = stat_send[place]

    for r in (2, 3, 1):
        stat_copy(r, True).start()
    own_stage(0)
    if stages > 1:
        start_in((0, 1), 1)
    start_in((2, 3), 0)
    for r in range(GROUP):
        if r:
            stat_copy(r, False).wait_recv()

        @pl.when(prev1)
        def _(r=r):
            stat_hop(0, nth(r)).start()

    for b in range(GROUP):
        seg = jnp.broadcast_to(stat[0, b, 8:9, :], (tok, tok))
        key_seg[b * tok : (b + 1) * tok, :] = seg.T

    def turn(i, carry):
        @pl.when(i + 1 < stages)
        def _():
            own_stage(i + 1)

        @pl.when(i + 2 < stages)
        def _():
            start_in((0, 1), i + 2)

        @pl.when((i < stages) & next1)
        def _():
            pl.when(i == 0)(stat_arrived)
            forward(i)

        @pl.when(i < stages)
        def _():
            own_work(i)

        @pl.when(i + 1 < stages)
        def _():
            start_in((2, 3), i + 1)

        @pl.when((i < stages) & next1)
        def _():
            next_work(i)

        @pl.when((i >= 1) & (i <= stages))
        def _():
            pl.when(next2)(functools.partial(last_work, i - 1))
            key_results(i - 1)

        @pl.when(i >= 2)
        def _():
            query_results(i - 2)

        return carry

    lax.fori_loop(0, stages + 2, turn, 0)

    for r in range(1, GROUP):
        stat_copy(r, True).wait_send()
    for b in range(GROUP):
        pl.when(prev1)(stat_hop(0, b).wait_send)
        if b < GROUP - 1:
            pl.when(prev1 & next1)(stat_hop(1, b).wait_send)

    def drain(s, carry):
        for a in range(3):
            out_own(a, s).wait()
        for r in range(1, GROUP):
            for a in range(4):
                in_copy(a, r, s, True).wait_send()
            for a in range(3):
                out_copy(a, r, s, True).wait_send()
                out_copy(a, r, s, False).wait_recv()
        for b in range(GROUP):
            pl.when(prev1)(hop_copy(0, b, s).wait_send)
            pl.when(next1)(dq_copy(0, b, s).wait_send)
            if b < GROUP - 1:
                pl.when(prev1 & next1)(hop_copy(1, b, s).wait_send)
                pl.when(next2)(dq_copy(1, b, s).wait_send)
        return carry

    lax.fori_loop(0, stages, drain, 0)


def on_device(queries, key_rows, value_rows, attn_out, out_grad, log_norm, segments):
    tok, width = queries.shape
    cols = width // GROUP
    stages = STAGES
    wide = cols // stages
    chain_len = lax.axis_size("ctx")
    bf16, f32 = jnp.bfloat16, jnp.float32
    dma = pltpu.SemaphoreType.DMA
    far = pl.BlockSpec(memory_space=pltpu.HBM)
    return pl.pallas_call(
        functools.partial(kernel, chain_len),
        out_shape=[jax.ShapeDtypeStruct((tok, width), bf16)] * 3,
        in_specs=[far] * 7,
        out_specs=[far] * 3,
        scratch_shapes=[
            pltpu.VMEM((tok, width), bf16),
            pltpu.VMEM((tok, width), bf16),
            pltpu.VMEM(log_norm.shape[::-1], f32),
            pltpu.VMEM((1, tok), jnp.int32),
            pltpu.VMEM((GROUP, 16, tok), f32),
            pltpu.VMEM((3, stages, GROUP, 2, tok, wide), bf16),
            pltpu.VMEM((3, GROUP, 16, tok), f32),
            pltpu.VMEM((stages, GROUP * tok, wide), bf16),
            pltpu.VMEM((stages, GROUP * tok, wide), bf16),
            pltpu.VMEM((GROUP * tok, tok), f32),
            pltpu.VMEM((stages, GROUP * tok, wide), f32),
            pltpu.VMEM((stages, GROUP * tok, wide), f32),
            pltpu.VMEM((stages, GROUP, tok, wide), f32),
            pltpu.VMEM((2, stages, GROUP, tok, wide), bf16),
            pltpu.VMEM((2, stages, GROUP, tok, wide), bf16),
            pltpu.VMEM((3, stages, GROUP, tok, wide), bf16),
            dma((5, max(stages, 4))),
            dma((3, GROUP)), dma((3, GROUP)),
            dma((4, GROUP, stages)), dma((4, GROUP, stages)),
            dma((2, GROUP, stages)), dma((2, GROUP, stages)),
            dma((2, GROUP, stages)), dma((2, GROUP, stages)),
            dma((3, GROUP, stages)), dma((3, GROUP, stages)),
        ],
        compiler_params=pltpu.CompilerParams(
            collective_id=0, has_side_effects=True, vmem_limit_bytes=62 * 1024 * 1024
        ),
        name="attention_backward",
    )(queries, key_rows, value_rows, attn_out, out_grad, log_norm.T, segments.reshape(1, tok))


def solution(mesh):
    placed = (P(("dp", "ctx"), None),) * 6 + (P(("dp", "ctx")),)
    return jax.shard_map(
        on_device,
        mesh=mesh,
        in_specs=placed,
        out_specs=(P(("dp", "ctx"), None),) * 3,
        check_vma=False,
    )
```
